32 devices in a mesh: sx: 4 (over y, x), sy: 2 (over core), sz: 4 (over z).
Axes of the slice: x: 2, y: 2, z: 4, core: 2. Of those that a mesh axis runs over, the one named last changes fastest.
Arguments:
- density: bfloat16 [4, 32, 16, 64], P(None, 'sx', 'sy', 'sz'), may hold values from -6 to 6
- conv1_weight: bfloat16 [32, 3, 3, 3, 4], replicated, may hold values from -0.625 to 0.625
- conv1_bias: float32 [32], replicated, may hold values from -3 to 3
- conv1_probe: bfloat16 [32, 3, 3, 3, 4], replicated, may hold values from -0.625 to 0.625
- conv2_weight: bfloat16 [32, 3, 3, 3, 32], replicated, may hold values from -0.21875 to 0.21875
- conv2_bias: float32 [32], replicated, may hold values from -3 to 3
- conv2_probe: bfloat16 [32, 3, 3, 3, 32], replicated, may hold values from -0.21875 to 0.21875
- lift_weight: bfloat16 [256, 4, 4, 4, 32], replicated, may hold values from -0.125 to 0.125
- lift_bias: float32 [256], replicated, may hold values from -3 to 3
- lift_probe: bfloat16 [256, 4, 4, 4, 32], replicated, may hold values from -0.125 to 0.125
- conv3_weight: bfloat16 [256, 3, 3, 3, 256], P(None, None, None, None, ('sx', 'sy')), may hold values from -0.109375 to 0.109375
- conv3_bias: float32 [256], P(('sx', 'sy')), may hold values from -3 to 3
- conv3_probe: bfloat16 [256, 3, 3, 3, 256], P(None, None, None, None, ('sx', 'sy')), may hold values from -0.109375 to 0.109375
Outputs:
- features: bfloat16 [256, 8, 4, 16], P(('sx', 'sy'), None, None, 'sz')
- tangent: bfloat16 [256, 8, 4, 16], P(('sx', 'sy'), None, None, 'sz')
The draws below stay inside these ranges and needn't reach their ends.
All inputs are finite; a program needn't handle non-finite values.
Results may differ from the reference program's by a relative error of at most 0.013.
Values may be sent and summed in bfloat16 or wider, within the bound.
A program may use at most 64 MiB of HBM per device.

```python
import jax
import jax.numpy as jnp
from jax import lax

CIN = 4
C1 = 32
C3 = 256
NX = 32
NY = 16
NZ = 64


def with_spikes(entries, rng, source, target, shards_of, factor):
    def block_of(axis_at):
        return (jnp.arange(entries.shape[axis_at]) // (entries.shape[axis_at] // shards_of)).reshape((-1,) + (1,) * (entries.ndim - 1 - axis_at))

    near = jax.random.permutation(rng, shards_of)[block_of(target)]
    far = (block_of(target) + shards_of // 2) % shards_of
    return jnp.where((block_of(source) == near) | (block_of(source) == far), factor * entries, entries)


def level_of(own_key, dims, shards, low, largest):
    level, own = 1.0, jax.random.fold_in(own_key, 6)
    for position, blocks in shards:
        steps = jnp.exp(jax.random.uniform(jax.random.fold_in(own, position), (blocks,), jnp.float32, low / len(shards), largest / len(shards)))
        level = level * jnp.repeat(steps, dims[position] // blocks).reshape([-1 if axis == position else 1 for axis in range(len(dims))])
    return level


def centred(stream_key, extent, width, bound, cuts=(), held_as=jnp.bfloat16):
    factor_of = level_of(stream_key, extent, cuts, -0.22, 0.18) if cuts else 1.0
    array = jax.random.normal(stream_key, extent, jnp.float32) * width * factor_of
    return jnp.minimum(jnp.maximum(array, -bound), bound).astype(held_as)


def heavy_noise(stream_key, dims, width, most, pieces, heavy, held_as=jnp.bfloat16):
    values = width * jax.random.normal(stream_key, dims, jnp.float32)
    if pieces:
        values = values * level_of(stream_key, dims, pieces, -0.22, 0.18)
    return jnp.clip(with_spikes(values, jax.random.fold_in(stream_key, 3), *heavy), -most, most).astype(held_as)


def setup_inputs(seed: int = 0) -> dict:
    streams_of = jax.random.split(jax.random.key(seed), 14)
    density = centred(streams_of[0], (CIN, NX, NY, NZ), 1.0, 6.0, ((1, 4), (2, 2), (3, 4)))
    conv1_weight = centred(streams_of[1], (C1, 3, 3, 3, CIN), (27 * CIN) ** -0.5, 0.625)
    conv1_bias = centred(streams_of[2], (C1,), 0.5, 3.0, (), jnp.float32)
    conv1_probe = centred(streams_of[3], (C1, 3, 3, 3, CIN), (27 * CIN) ** -0.5, 0.625)
    conv2_weight = centred(streams_of[4], (C1, 3, 3, 3, C1), (27 * C1) ** -0.5, 0.21875)
    conv2_bias = centred(streams_of[5], (C1,), 0.5, 3.0, (), jnp.float32)
    conv2_probe = centred(streams_of[6], (C1, 3, 3, 3, C1), (27 * C1) ** -0.5, 0.21875)
    lift_weight = centred(streams_of[7], (C3, 4, 4, 4, C1), (64 * C1) ** -0.5, 0.125)
    lift_bias = centred(streams_of[8], (C3,), 0.5, 3.0, (), jnp.float32)
    lift_probe = centred(streams_of[9], (C3, 4, 4, 4, C1), (64 * C1) ** -0.5, 0.125)
    conv3_weight = heavy_noise(streams_of[10], (C3, 3, 3, 3, C3), (27 * C3) ** -0.5, 0.109375, ((4, 8),), (4, 0, 8, 2.0))
    conv3_bias = centred(streams_of[11], (C3,), 0.5, 3.0, ((0, 8),), jnp.float32)
    conv3_probe = heavy_noise(streams_of[12], (C3, 3, 3, 3, C3), (27 * C3) ** -0.5, 0.109375, ((4, 8),), (4, 0, 8, 2.0))
    return {"density": density, "conv1_weight": conv1_weight, "conv1_bias": conv1_bias, "conv1_probe": conv1_probe, "conv2_weight": conv2_weight, "conv2_bias": conv2_bias, "conv2_probe": conv2_probe, "lift_weight": lift_weight, "lift_bias": lift_bias, "lift_probe": lift_probe, "conv3_weight": conv3_weight, "conv3_bias": conv3_bias, "conv3_probe": conv3_probe}


def swish_pair(preact, direction):
    sigmoid_value = jax.nn.sigmoid(preact)
    derivative = sigmoid_value * (1.0 + preact * (1.0 - sigmoid_value))
    return preact * sigmoid_value, derivative * direction


def convolve(volume, weight, stride, padding):
    kernel = jnp.transpose(weight, (0, 4, 1, 2, 3)).astype(jnp.float32)
    result = lax.conv_general_dilated(volume.astype(jnp.float32)[None], kernel, (stride, stride, stride), padding, dimension_numbers=("NCDHW", "OIDHW", "NCDHW"), precision=lax.Precision.HIGHEST, preferred_element_type=jnp.float32)
    return result[0]


def layer(hidden, probe, weight, bias, weight_probe, stride, padding):
    preact = convolve(hidden, weight, stride, padding) + bias[:, None, None, None]
    change = convolve(hidden, weight_probe, stride, padding)
    if probe is not None:
        change = change + convolve(probe, weight, stride, padding)
    return preact, change


def reference(density, conv1_weight, conv1_bias, conv1_probe, conv2_weight, conv2_bias, conv2_probe, lift_weight, lift_bias, lift_probe, conv3_weight, conv3_bias, conv3_probe):
    preact, change = layer(density, None, conv1_weight, conv1_bias, conv1_probe, 1, "SAME")
    hidden, probe = swish_pair(preact, change)
    hidden = hidden.astype(jnp.bfloat16)
    probe = probe.astype(jnp.bfloat16)
    preact, change = layer(hidden, probe, conv2_weight, conv2_bias, conv2_probe, 1, "SAME")
    hidden, probe = swish_pair(preact, change)
    hidden = hidden.astype(jnp.bfloat16)
    probe = probe.astype(jnp.bfloat16)
    preact, change = layer(hidden, probe, lift_weight, lift_bias, lift_probe, 4, "VALID")
    hidden, probe = swish_pair(preact, change)
    hidden = hidden.astype(jnp.bfloat16)
    probe = probe.astype(jnp.bfloat16)
    preact, change = layer(hidden, probe, conv3_weight, conv3_bias, conv3_probe, 1, "SAME")
    return preact.astype(jnp.bfloat16), change.astype(jnp.bfloat16)
```

```python
import functools
import itertools

import jax
import jax.numpy as jnp
from jax import lax
from jax.experimental import pallas as pl
from jax.experimental.pallas import tpu as pltpu
from jax.sharding import PartitionSpec as P

MESH = pl.DeviceIdType.MESH
VMEM = pl.BlockSpec(memory_space=pltpu.VMEM)


def swish_pair(preact, direction):
    sigmoid_value = jax.nn.sigmoid(preact)
    derivative = sigmoid_value * (1.0 + preact * (1.0 - sigmoid_value))
    return (preact * sigmoid_value, derivative * direction)


def cells(volume, weight, stride, out_order):
    return lax.conv_general_dilated(
        volume,
        weight,
        (stride, stride, stride),
        "VALID",
        dimension_numbers=("NCDHW", "ODHWI", out_order),
        preferred_element_type=jnp.float32,
    )


def per_channel(vector):
    return vector[:, None, None, None]


def inside_range(length, offset, whole):
    position = jnp.arange(length, dtype=jnp.int32) - 1 + offset
    return ((position >= 0) & (position < whole)).astype(jnp.float32)


def positions(axes):
    return [lax.axis_index(a) for a in axes], [lax.axis_size(a) for a in axes]


OFFSETS = list(itertools.product((-1, 0, 1), repeat=3))


def one_hot(rows, columns, source, dim):
    shape = (rows, 1) if dim == 0 else (1, columns)
    want, ok = source(lax.broadcasted_iota(jnp.int32, shape, dim))
    want = jnp.where(ok, want, -1)
    return (lax.broadcasted_iota(jnp.int32, (rows, columns), 1 - dim) == want).astype(jnp.bfloat16)


def tiles_kernel(shape, width, tile, out, slots, send_sem, recv_sem):
    channels, span_x, span_y, span_z = shape
    wide_x, wide_y, wide_z = (span + 2 * width for span in (span_x, span_y, span_z))
    axes = ("sx", "sy", "sz")
    at, counts = positions(axes)

    def there(offset):
        ok = None
        for here, step, count in zip(at, offset, counts):
            if step:
                one = (here + step >= 0) & (here + step < count)
                ok = one if ok is None else ok & one
        return ok, tuple(here + step for here, step in zip(at, offset))

    others = [(i, o) for i, o in enumerate(OFFSETS) if any(o)]
    barrier = pltpu.get_barrier_semaphore()
    for _, offset in others:
        ok, target = there(offset)

        @pl.when(ok)
        def _():
            pl.semaphore_signal(barrier, inc=1, device_id=target, device_id_type=MESH)

    peers = 1
    for here, count in zip(at, counts):
        peers *= 1 + (here > 0).astype(jnp.int32) + (here < count - 1).astype(jnp.int32)
    pl.semaphore_wait(barrier, peers - 1)

    def copy(i, offset, target):
        return pltpu.make_async_remote_copy(
            src_ref=tile,
            dst_ref=slots.at[len(OFFSETS) - 1 - i],
            send_sem=send_sem.at[i],
            recv_sem=recv_sem.at[len(OFFSETS) - 1 - i],
            device_id=target,
            device_id_type=MESH,
        )

    for i, offset in others:
        ok, target = there(offset)

        @pl.when(ok)
        def _():
            copy(i, offset, target).start()

    slots[len(OFFSETS) // 2] = tile[...]
    cells_in = span_y * span_z

    def column(at_row):
        block, cell = at_row // cells_in, at_row % cells_in
        y = cell // span_z + width + (block // 3 - 1) * span_y
        z = cell % span_z + width + (block % 3 - 1) * span_z
        return y * wide_z + z, (y >= 0) & (y < wide_y) & (z >= 0) & (z < wide_z)

    def line(at_column):
        block, cell = at_column // (channels * span_x), at_column % (channels * span_x)
        x = cell % span_x + width + (block - 1) * span_x
        return cell // span_x * wide_x + x, (x >= 0) & (x < wide_x)

    columns = one_hot(9 * cells_in, wide_y * wide_z, column, 0)
    lines = one_hot(channels * wide_x, 3 * channels * span_x, line, 1)
    for i, offset in others:
        ok, target = there(offset)

        @pl.when(ok)
        def _():
            mirror = len(OFFSETS) - 1 - i
            copy(mirror, offset, target).wait_recv()

        @pl.when(jnp.logical_not(ok))
        def _():
            slots[i] = jnp.zeros_like(tile)

    dot = functools.partial(jnp.dot, preferred_element_type=jnp.float32)
    near = jnp.concatenate(
        [jnp.concatenate([slots[9 * i + j] for j in range(9)], axis=1) for i in range(3)], axis=0
    )
    near = dot(near, columns).astype(jnp.bfloat16)
    out[...] = dot(lines, near).astype(jnp.bfloat16)
    for i, offset in others:
        ok, target = there(offset)

        @pl.when(ok)
        def _():
            copy(i, offset, target).wait_send()


def with_halo(tile, width):
    channels, span_x, span_y, span_z = tile.shape
    wide_x, wide_y, wide_z = (span + 2 * width for span in (span_x, span_y, span_z))
    flat = (channels * span_x, span_y * span_z)
    return pl.pallas_call(
        functools.partial(tiles_kernel, tile.shape, width),
        out_shape=jax.ShapeDtypeStruct((channels * wide_x, wide_y * wide_z), tile.dtype),
        in_specs=[VMEM],
        out_specs=VMEM,
        scratch_shapes=[
            pltpu.VMEM((len(OFFSETS),) + flat, tile.dtype),
            pltpu.SemaphoreType.DMA((len(OFFSETS),)),
            pltpu.SemaphoreType.DMA((len(OFFSETS),)),
        ],
        compiler_params=pltpu.CompilerParams(collective_id=0, has_side_effects=True),
    )(tile.reshape(flat)).reshape(channels, wide_x, wide_y, wide_z)


def last_kernel(
    tile_shape, blocks, weight, probe, bias, out, lifted, sent, rows, copies, parts, landed,
    lift_send, lift_recv, part_send, part_recv,
):
    tx, ty, tz = tile_shape
    (ix, iy, iz), (nx, ny, nz) = positions(("sx", "sy", "sz"))
    groups = nx * ny
    me = ix * ny + iy
    width = weight.shape[0] // 27
    whole_y, depth = ny * ty, tz + 2
    step_y, step_x = depth, depth * (whole_y + 1)
    count = sent.shape[1]
    owned = out.shape[1]

    def place(k, dz):
        group = lax.rem(me + k, groups)
        return group, (lax.div(group, ny), lax.rem(group, ny), iz + dz)

    plan = [(dz, k) for dz in (0, -1, 1) for k in range(groups) if k or dz]

    def guarded(dz, action):
        if dz == 0:
            action()
        else:
            pl.when((iz + dz >= 0) & (iz + dz < nz))(action)

    barrier = pltpu.get_barrier_semaphore()

    def greet(dz):
        for k in range(groups):
            if k or dz:
                _, target = place(k, dz)
                pl.semaphore_signal(barrier, inc=1, device_id=target, device_id_type=MESH)

    for dz in (0, -1, 1):
        guarded(dz, functools.partial(greet, dz))
    slabs = 1 + (iz > 0).astype(jnp.int32) + (iz < nz - 1).astype(jnp.int32)
    pl.semaphore_wait(barrier, groups * slabs - 1)

    def lift_copy(dz, k):
        group, target = place(k, dz)
        return pltpu.make_async_remote_copy(
            src_ref=blocks.at[group],
            dst_ref=lifted.at[1 - dz, me],
            send_sem=lift_send.at[1 + dz, k],
            recv_sem=lift_recv.at[1 - dz, me],
            device_id=target,
            device_id_type=MESH,
        )

    def arrival(dz, group):
        return pltpu.make_async_remote_copy(
            src_ref=blocks.at[group],
            dst_ref=lifted.at[1 + dz, group],
            send_sem=lift_send.at[1 + dz, 0],
            recv_sem=lift_recv.at[1 + dz, group],
            device_id=(lax.div(group, ny), lax.rem(group, ny), iz),
            device_id_type=MESH,
        )

    def launch(dz):
        for k in range(groups):
            if k or dz:
                lift_copy(dz, k).start()

    for dz in (0, -1, 1):
        guarded(dz, functools.partial(launch, dz))

    lifted[1, me] = blocks[me]
    rows[...] = jnp.zeros_like(rows)

    def row_of(x, y, z):
        return (x + 1) * step_x + (y + 1) * step_y + z + 1

    def land(dz):
        for k in range(groups):
            if k or dz:
                arrival(dz, lax.rem(me + k, groups)).wait_recv()
        for group in range(groups):
            gx, gy = group // ny, group % ny
            block = lifted[1 + dz, group].astype(jnp.float32)
            for i in range(tx):
                for j in range(ty):
                    start = (i * ty + j) * tz
                    first, size, z = {0: (0, tz, 0), -1: (tz - 1, 1, -1), 1: (0, 1, tz)}[dz]
                    target = row_of(gx * tx + i, gy * ty + j, z)
                    rows[target : target + size, 0 : 2 * width] = block[
                        start + first : start + first + size
                    ]

    for dz in (0, -1, 1):
        guarded(dz, functools.partial(land, dz))

    lanes = rows.shape[1]
    per = lanes // width
    lane = lax.broadcasted_iota(jnp.int32, rows.shape, 1) // width
    full = rows[...]
    for which in range(2):
        for k in range(per):
            shift = (k - which) * width % lanes
            turned = pltpu.roll(full, shift, 1) if shift else full
            copies[which * per + k] = jnp.where(lane == k, turned, 0.0)

    taps = [p * step_x + q * step_y + r for p in range(3) for q in range(3) for r in range(3)]

    def patches(which):
        chunks = []
        for first in range(0, 27, per):
            chunk = None
            for k, tap in enumerate(taps[first : first + per]):
                window = copies[which * per + k, tap : tap + count]
                chunk = window if chunk is None else chunk + window
            chunks.append(chunk.astype(jnp.bfloat16))
        return jnp.concatenate(chunks, axis=1)[:, : 27 * width]

    hidden, change = patches(0), patches(1)
    dot = functools.partial(jnp.dot, preferred_element_type=jnp.float32)
    primal = dot(hidden, weight[...])
    tangent = dot(hidden, probe[...]) + dot(change, weight[...])

    cellcount = out.shape[2]
    row = lax.broadcasted_iota(jnp.int32, (count, cellcount), 0)
    cell = lax.broadcasted_iota(jnp.int32, (count, cellcount), 1)
    source = (
        cell // (whole_y * tz) * step_x + cell // tz % whole_y * step_y + cell % tz
    )
    pick = (row == source).astype(jnp.bfloat16)
    for which, value in enumerate((primal, tangent)):
        dense = dot(value.T.astype(jnp.bfloat16), pick).astype(jnp.bfloat16)
        for group in range(groups):
            parts[group, which] = dense[group * owned : (group + 1) * owned]

    def part_copy(k):
        group, target = place(k, 0)
        return pltpu.make_async_remote_copy(
            src_ref=parts.at[group],
            dst_ref=landed.at[me],
            send_sem=part_send.at[k],
            recv_sem=part_recv.at[me],
            device_id=target,
            device_id_type=MESH,
        )

    def part_arrival(k):
        group, target = place(k, 0)
        return pltpu.make_async_remote_copy(
            src_ref=parts.at[group],
            dst_ref=landed.at[group],
            send_sem=part_send.at[k],
            recv_sem=part_recv.at[group],
            device_id=target,
            device_id_type=MESH,
        )

    for k in range(1, groups):
        part_copy(k).start()
    total = parts[me].astype(jnp.float32)
    for k in range(1, groups):
        part_arrival(k).wait_recv()
        total = total + landed[lax.rem(me + k, groups)].astype(jnp.float32)
    out[0] = (total[0] + bias[...]).astype(out.dtype)
    out[1] = total[1].astype(out.dtype)
    for dz, k in plan:
        guarded(dz, lambda: lift_copy(dz, k).wait_send())
    for k in range(1, groups):
        part_copy(k).wait_send()


def last_layer(blocks, weight, probe, bias, tile_shape):
    tx, ty, tz = tile_shape
    (nx, ny) = lax.axis_size("sx"), lax.axis_size("sy")
    groups, cells_in, pair_width = blocks.shape
    width = pair_width // 2
    outputs = weight.shape[1]
    owned = outputs // groups
    step_x = (ny * ty + 1) * (tz + 2)
    count = -(-nx * tx * step_x // 128) * 128
    height = -(-(count + 2 * step_x + 2 * (tz + 2) + 2) // 16) * 16
    cellcount = nx * tx * ny * ty * tz
    lanes = 128
    per = lanes // width
    bf16, f32 = jnp.bfloat16, jnp.float32
    return pl.pallas_call(
        functools.partial(last_kernel, tile_shape),
        out_shape=jax.ShapeDtypeStruct((2, owned, cellcount), bf16),
        in_specs=[VMEM] * 4,
        out_specs=VMEM,
        scratch_shapes=[
            pltpu.VMEM((3, groups, cells_in, pair_width), bf16),
            pltpu.VMEM((1, count, 128), bf16),
            pltpu.VMEM((height, lanes), f32),
            pltpu.VMEM((2 * per, height, lanes), f32),
            pltpu.VMEM((groups, 2, owned, cellcount), bf16),
            pltpu.VMEM((groups, 2, owned, cellcount), bf16),
            pltpu.SemaphoreType.DMA((3, groups)),
            pltpu.SemaphoreType.DMA((3, groups)),
            pltpu.SemaphoreType.DMA((groups,)),
            pltpu.SemaphoreType.DMA((groups,)),
        ],
        compiler_params=pltpu.CompilerParams(
            collective_id=1, has_side_effects=True, vmem_limit_bytes=48 * 2**20
        ),
    )(blocks, weight, probe, bias)


def flat_weight(weight):
    outputs = weight.shape[0]
    return jnp.transpose(weight, (1, 2, 3, 4, 0)).reshape(-1, outputs)


def body(
    density,
    conv1_weight,
    conv1_bias,
    conv1_probe,
    conv2_weight,
    conv2_bias,
    conv2_probe,
    lift_weight,
    lift_bias,
    lift_probe,
    conv3_weight,
    conv3_bias,
    conv3_probe,
):
    channels_in, span_x, span_y, span_z = density.shape
    width_one = conv1_weight.shape[0]
    width_three = lift_weight.shape[0]
    both_first = jnp.concatenate([conv1_weight, conv1_probe], 0)
    padded = with_halo(density, 2)
    pre_both = cells(padded[None], both_first, 1, "NCDHW")[0]
    hidden, probe = swish_pair(pre_both[:width_one] + per_channel(conv1_bias), pre_both[width_one:])
    inside_x = inside_range(span_x + 2, lax.axis_index("sx") * span_x, span_x * lax.axis_size("sx"))
    inside_y = inside_range(span_y + 2, lax.axis_index("sy") * span_y, span_y * lax.axis_size("sy"))
    inside_z = inside_range(span_z + 2, lax.axis_index("sz") * span_z, span_z * lax.axis_size("sz"))
    inside = inside_x[:, None, None] * inside_y[None, :, None] * inside_z[None, None, :]
    pair = jnp.stack(
        [(hidden * inside).astype(jnp.bfloat16), (probe * inside).astype(jnp.bfloat16)]
    )
    both = cells(pair, conv2_weight, 1, "NCDHW")
    extra = cells(pair[:1], conv2_probe, 1, "NCDHW")[0]
    hidden, probe = swish_pair(both[0] + per_channel(conv2_bias), both[1] + extra)
    pair = jnp.stack([hidden.astype(jnp.bfloat16), probe.astype(jnp.bfloat16)])
    both = cells(pair, lift_weight, 4, "NDHWC")
    extra = cells(pair[:1], lift_probe, 4, "NDHWC")[0]
    hidden, probe = swish_pair(both[0] + lift_bias, both[1] + extra)
    stacked = jnp.stack([hidden.astype(jnp.bfloat16), probe.astype(jnp.bfloat16)])
    tile_shape = stacked.shape[1:4]
    groups = lax.axis_size("sx") * lax.axis_size("sy")
    width = width_three // groups
    blocks = stacked.reshape(2, -1, groups, width)
    blocks = jnp.transpose(blocks, (2, 1, 0, 3)).reshape(groups, -1, 2 * width)
    result = last_layer(
        blocks, flat_weight(conv3_weight), flat_weight(conv3_probe), conv3_bias[:, None], tile_shape
    )
    tx, ty, tz = tile_shape
    result = result.reshape(
        2, -1, tx * lax.axis_size("sx"), ty * lax.axis_size("sy"), tz
    )
    return (result[0], result[1])


def solution(mesh):
    placed = (
        P(None, "sx", "sy", "sz"),
        P(),
        P(),
        P(),
        P(),
        P(),
        P(),
        P(),
        P(),
        P(),
        P(None, None, None, None, ("sx", "sy")),
        P(("sx", "sy")),
        P(None, None, None, None, ("sx", "sy")),
    )
    return jax.shard_map(
        body,
        mesh=mesh,
        in_specs=placed,
        out_specs=(P(("sx", "sy"), None, None, "sz"), P(("sx", "sy"), None, None, "sz")),
        check_vma=False,
    )
```

```python
import functools
import itertools

import jax
import jax.numpy as jnp
from jax import lax
from jax.experimental import pallas as pl
from jax.experimental.pallas import tpu as pltpu
from jax.sharding import PartitionSpec as P

MESH = pl.DeviceIdType.MESH
VMEM = pl.BlockSpec(memory_space=pltpu.VMEM)


def swish_pair(preact, direction):
    sigmoid_value = jax.nn.sigmoid(preact)
    derivative = sigmoid_value * (1.0 + preact * (1.0 - sigmoid_value))
    return (preact * sigmoid_value, derivative * direction)


def cells(volume, weight, stride, out_order):
    return lax.conv_general_dilated(
        volume,
        weight,
        (stride, stride, stride),
        "VALID",
        dimension_numbers=("NDHWC", "ODHWI", out_order),
        preferred_element_type=jnp.float32,
    )


def positions(axes):
    return [lax.axis_index(a) for a in axes], [lax.axis_size(a) for a in axes]


OFFSETS = list(itertools.product((-1, 0, 1), repeat=3))


def one_hot(rows, columns, source, dim):
    shape = (rows, 1) if dim == 0 else (1, columns)
    want, ok = source(lax.broadcasted_iota(jnp.int32, shape, dim))
    want = jnp.where(ok, want, -1)
    return (lax.broadcasted_iota(jnp.int32, (rows, columns), 1 - dim) == want).astype(jnp.bfloat16)


def tiles_kernel(
    shape, tile, weight1, bias1, weight2, bias2, out, slots, flat, send_sem, recv_sem
):
    width = 2
    channels, span_x, span_y, span_z = shape
    wide_x, wide_y, wide_z = (span + 2 * width for span in (span_x, span_y, span_z))
    axes = ("sx", "sy", "sz")
    at, counts = positions(axes)

    def there(offset):
        ok = None
        for here, step, count in zip(at, offset, counts):
            if step:
                one = (here + step >= 0) & (here + step < count)
                ok = one if ok is None else ok & one
        return ok, tuple(here + step for here, step in zip(at, offset))

    others = [(i, o) for i, o in enumerate(OFFSETS) if any(o)]
    barrier = pltpu.get_barrier_semaphore()
    for _, offset in others:
        ok, target = there(offset)

        @pl.when(ok)
        def _():
            pl.semaphore_signal(barrier, inc=1, device_id=target, device_id_type=MESH)

    peers = 1
    for here, count in zip(at, counts):
        peers *= 1 + (here > 0).astype(jnp.int32) + (here < count - 1).astype(jnp.int32)
    pl.semaphore_wait(barrier, peers - 1)

    def copy(i, offset, target):
        return pltpu.make_async_remote_copy(
            src_ref=tile,
            dst_ref=slots.at[len(OFFSETS) - 1 - i],
            send_sem=send_sem.at[i],
            recv_sem=recv_sem.at[len(OFFSETS) - 1 - i],
            device_id=target,
            device_id_type=MESH,
        )

    for i, offset in others:
        ok, target = there(offset)

        @pl.when(ok)
        def _():
            copy(i, offset, target).start()

    slots[len(OFFSETS) // 2] = tile[...]
    cells_in = span_y * span_z

    def column(at_row):
        block, cell = at_row // cells_in, at_row % cells_in
        y = cell // span_z + width + (block // 3 - 1) * span_y
        z = cell % span_z + width + (block % 3 - 1) * span_z
        return y * wide_z + z, (y >= 0) & (y < wide_y) & (z >= 0) & (z < wide_z)

    def line(at_column):
        block, cell = at_column // (channels * span_x), at_column % (channels * span_x)
        x = cell % span_x + width + (block - 1) * span_x
        return x * deep + cell // span_x, (x >= 0) & (x < wide_x)

    pitch = -(-wide_y * wide_z // 128) * 128
    deep = weight1.shape[1] // 27
    columns = one_hot(9 * cells_in, pitch, column, 0)
    lines = one_hot(deep * wide_x, 3 * channels * span_x, line, 1)
    for i, offset in others:
        ok, target = there(offset)

        @pl.when(ok)
        def _():
            mirror = len(OFFSETS) - 1 - i
            copy(mirror, offset, target).wait_recv()

        @pl.when(jnp.logical_not(ok))
        def _():
            slots[i] = jnp.zeros_like(tile)

    dot = functools.partial(jnp.dot, preferred_element_type=jnp.float32)
    near = jnp.concatenate(
        [jnp.concatenate([slots[9 * i + j] for j in range(9)], axis=1) for i in range(3)], axis=0
    )
    near = dot(near, columns).astype(jnp.bfloat16)
    near = dot(lines, near)
    field = jnp.concatenate([near[deep * x : deep * (x + 1)] for x in range(wide_x)], axis=1)

    def patches(values):
        lanes = values.shape[1]
        taps = []
        for q in range(3):
            for r in range(3):
                shift = -((q - 1) * wide_z + r - 1) % lanes
                taps.append(pltpu.roll(values, shift, 1) if shift else values)
        kept = lanes - 2 * pitch
        return jnp.concatenate(
            [tap[:, p * pitch : p * pitch + kept] for p in range(3) for tap in taps], axis=0
        ).astype(jnp.bfloat16)

    width_one = weight1.shape[0] // 2
    both = dot(weight1[...], patches(field))
    hidden, probe = swish_pair(both[:width_one] + bias1[...], both[width_one:])
    place = lax.broadcasted_iota(jnp.int32, (1, hidden.shape[1]), 1)
    cell = place % pitch
    inside = None
    for here, count, span, index in zip(
        at, counts, (span_x, span_y, span_z), (place // pitch + 1, cell // wide_z, cell % wide_z)
    ):
        index = index - width + here * span
        one = (index >= 0) & (index < count * span)
        inside = one if inside is None else inside & one
    hidden = patches(jnp.where(inside, hidden, 0.0))
    probe = patches(jnp.where(inside, probe, 0.0))
    both = dot(weight2[...], hidden)
    change = both[width_one:] + dot(weight2[:width_one], probe)
    hidden, probe = swish_pair(both[:width_one] + bias2[...], change)
    flat[...] = jnp.concatenate([hidden, probe], axis=0).T
    for x in range(span_x):
        for y in range(span_y):
            start = x * pitch + (y + width) * wide_z + width
            to = (x * span_y + y) * span_z
            out[to : to + span_z] = flat[start : start + span_z].astype(jnp.bfloat16)
    for i, offset in others:
        ok, target = there(offset)

        @pl.when(ok)
        def _():
            copy(i, offset, target).wait_send()


def first_layers(tile, weight1, bias1, weight2, bias2):
    channels, span_x, span_y, span_z = tile.shape
    merged = (channels * span_x, span_y * span_z)
    pitch = -(-(span_y + 4) * (span_z + 4) // 128) * 128
    pair_width = weight1.shape[0]
    return pl.pallas_call(
        functools.partial(tiles_kernel, tile.shape),
        out_shape=jax.ShapeDtypeStruct((span_x * span_y * span_z, pair_width), tile.dtype),
        in_specs=[VMEM] * 5,
        out_specs=VMEM,
        scratch_shapes=[
            pltpu.VMEM((len(OFFSETS),) + merged, tile.dtype),
            pltpu.VMEM((span_x * pitch, pair_width), jnp.float32),
            pltpu.SemaphoreType.DMA((len(OFFSETS),)),
            pltpu.SemaphoreType.DMA((len(OFFSETS),)),
        ],
        compiler_params=pltpu.CompilerParams(
            collective_id=0, has_side_effects=True, vmem_limit_bytes=48 * 2**20
        ),
    )(tile.reshape(merged), weight1, bias1, weight2, bias2)


def last_kernel(
    tile_shape, blocks, weight, probe, bias, out, lifted, sent, rows, copies, parts, landed,
    lift_send, lift_recv, part_send, part_recv,
):
    tx, ty, tz = tile_shape
    (ix, iy, iz), (nx, ny, nz) = positions(("sx", "sy", "sz"))
    groups = nx * ny
    me = ix * ny + iy
    width = weight.shape[0] // 27
    whole_y, depth = ny * ty, tz + 2
    step_y, step_x = depth, depth * (whole_y + 1)
    count = sent.shape[1]
    owned = out.shape[1]

    def place(k, dz):
        group = lax.rem(me + k, groups)
        return group, (lax.div(group, ny), lax.rem(group, ny), iz + dz)

    plan = [(dz, k) for dz in (0, -1, 1) for k in range(groups) if k or dz]

    def guarded(dz, action):
        if dz == 0:
            action()
        else:
            pl.when((iz + dz >= 0) & (iz + dz < nz))(action)

    barrier = pltpu.get_barrier_semaphore()

    def greet(dz):
        for k in range(groups):
            if k or dz:
                _, target = place(k, dz)
                pl.semaphore_signal(barrier, inc=1, device_id=target, device_id_type=MESH)

    for dz in (0, -1, 1):
        guarded(dz, functools.partial(greet, dz))
    slabs = 1 + (iz > 0).astype(jnp.int32) + (iz < nz - 1).astype(jnp.int32)
    pl.semaphore_wait(barrier, groups * slabs - 1)

    def lift_copy(dz, k):
        group, target = place(k, dz)
        return pltpu.make_async_remote_copy(
            src_ref=blocks.at[group],
            dst_ref=lifted.at[1 - dz, me],
            send_sem=lift_send.at[1 + dz, k],
            recv_sem=lift_recv.at[1 - dz, me],
            device_id=target,
            device_id_type=MESH,
        )

    def arrival(dz, group):
        return pltpu.make_async_remote_copy(
            src_ref=blocks.at[group],
            dst_ref=lifted.at[1 + dz, group],
            send_sem=lift_send.at[1 + dz, 0],
            recv_sem=lift_recv.at[1 + dz, group],
            device_id=(lax.div(group, ny), lax.rem(group, ny), iz),
            device_id_type=MESH,
        )

    def launch(dz):
        for k in range(groups):
            if k or dz:
                lift_copy(dz, k).start()

    for dz in (0, -1, 1):
        guarded(dz, functools.partial(launch, dz))

    lifted[1, me] = blocks[me]
    rows[...] = jnp.zeros_like(rows)

    def row_of(x, y, z):
        return (x + 1) * step_x + (y + 1) * step_y + z + 1

    def land(dz):
        for k in range(groups):
            if k or dz:
                arrival(dz, lax.rem(me + k, groups)).wait_recv()
        for group in range(groups):
            gx, gy = group // ny, group % ny
            block = lifted[1 + dz, group].astype(jnp.float32)
            for i in range(tx):
                for j in range(ty):
                    start = (i * ty + j) * tz
                    first, size, z = {0: (0, tz, 0), -1: (tz - 1, 1, -1), 1: (0, 1, tz)}[dz]
                    target = row_of(gx * tx + i, gy * ty + j, z)
                    rows[target : target + size, 0 : 2 * width] = block[
                        start + first : start + first + size
                    ]

    for dz in (0, -1, 1):
        guarded(dz, functools.partial(land, dz))

    lanes = rows.shape[1]
    per = lanes // width
    lane = lax.broadcasted_iota(jnp.int32, rows.shape, 1) // width
    full = rows[...]
    for which in range(2):
        for k in range(per):
            shift = (k - which) * width % lanes
            turned = pltpu.roll(full, shift, 1) if shift else full
            copies[which * per + k] = jnp.where(lane == k, turned, 0.0)

    taps = [p * step_x + q * step_y + r for p in range(3) for q in range(3) for r in range(3)]

    def patches(which):
        chunks = []
        for first in range(0, 27, per):
            chunk = None
            for k, tap in enumerate(taps[first : first + per]):
                window = copies[which * per + k, tap : tap + count]
                chunk = window if chunk is None else chunk + window
            chunks.append(chunk.astype(jnp.bfloat16))
        return jnp.concatenate(chunks, axis=1)[:, : 27 * width]

    hidden, change = patches(0), patches(1)
    dot = functools.partial(jnp.dot, preferred_element_type=jnp.float32)
    primal = dot(hidden, weight[...])
    tangent = dot(hidden, probe[...]) + dot(change, weight[...])

    cellcount = out.shape[2]
    row = lax.broadcasted_iota(jnp.int32, (count, cellcount), 0)
    cell = lax.broadcasted_iota(jnp.int32, (count, cellcount), 1)
    source = (
        cell // (whole_y * tz) * step_x + cell // tz % whole_y * step_y + cell % tz
    )
    pick = (row == source).astype(jnp.bfloat16)
    for which, value in enumerate((primal, tangent)):
        dense = dot(value.T.astype(jnp.bfloat16), pick).astype(jnp.bfloat16)
        for group in range(groups):
            parts[group, which] = dense[group * owned : (group + 1) * owned]

    def part_copy(k):
        group, target = place(k, 0)
        return pltpu.make_async_remote_copy(
            src_ref=parts.at[group],
            dst_ref=landed.at[me],
            send_sem=part_send.at[k],
            recv_sem=part_recv.at[me],
            device_id=target,
            device_id_type=MESH,
        )

    def part_arrival(k):
        group, target = place(k, 0)
        return pltpu.make_async_remote_copy(
            src_ref=parts.at[group],
            dst_ref=landed.at[group],
            send_sem=part_send.at[k],
            recv_sem=part_recv.at[group],
            device_id=target,
            device_id_type=MESH,
        )

    for k in range(1, groups):
        part_copy(k).start()
    total = parts[me].astype(jnp.float32)
    for k in range(1, groups):
        part_arrival(k).wait_recv()
        total = total + landed[lax.rem(me + k, groups)].astype(jnp.float32)
    out[0] = (total[0] + bias[...]).astype(out.dtype)
    out[1] = total[1].astype(out.dtype)
    for dz, k in plan:
        guarded(dz, lambda: lift_copy(dz, k).wait_send())
    for k in range(1, groups):
        part_copy(k).wait_send()


def last_layer(blocks, weight, probe, bias, tile_shape):
    tx, ty, tz = tile_shape
    (nx, ny) = lax.axis_size("sx"), lax.axis_size("sy")
    groups, cells_in, pair_width = blocks.shape
    width = pair_width // 2
    outputs = weight.shape[1]
    owned = outputs // groups
    step_x = (ny * ty + 1) * (tz + 2)
    count = -(-nx * tx * step_x // 128) * 128
    height = -(-(count + 2 * step_x + 2 * (tz + 2) + 2) // 16) * 16
    cellcount = nx * tx * ny * ty * tz
    lanes = 128
    per = lanes // width
    bf16, f32 = jnp.bfloat16, jnp.float32
    return pl.pallas_call(
        functools.partial(last_kernel, tile_shape),
        out_shape=jax.ShapeDtypeStruct((2, owned, cellcount), bf16),
        in_specs=[VMEM] * 4,
        out_specs=VMEM,
        scratch_shapes=[
            pltpu.VMEM((3, groups, cells_in, pair_width), bf16),
            pltpu.VMEM((1, count, 128), bf16),
            pltpu.VMEM((height, lanes), f32),
            pltpu.VMEM((2 * per, height, lanes), f32),
            pltpu.VMEM((groups, 2, owned, cellcount), bf16),
            pltpu.VMEM((groups, 2, owned, cellcount), bf16),
            pltpu.SemaphoreType.DMA((3, groups)),
            pltpu.SemaphoreType.DMA((3, groups)),
            pltpu.SemaphoreType.DMA((groups,)),
            pltpu.SemaphoreType.DMA((groups,)),
        ],
        compiler_params=pltpu.CompilerParams(
            collective_id=1, has_side_effects=True, vmem_limit_bytes=48 * 2**20
        ),
    )(blocks, weight, probe, bias)


def flat_weight(weight):
    outputs = weight.shape[0]
    return jnp.transpose(weight, (1, 2, 3, 4, 0)).reshape(-1, outputs)


def body(
    density,
    conv1_weight,
    conv1_bias,
    conv1_probe,
    conv2_weight,
    conv2_bias,
    conv2_probe,
    lift_weight,
    lift_bias,
    lift_probe,
    conv3_weight,
    conv3_bias,
    conv3_probe,
):
    channels_in, span_x, span_y, span_z = density.shape
    width_one = conv1_weight.shape[0]
    width_three = lift_weight.shape[0]
    both_first = jnp.concatenate([conv1_weight, conv1_probe], 0)
    spare = -channels_in % 8
    both_first = jnp.pad(both_first, ((0, 0),) * 4 + ((0, spare),)).reshape(2 * width_one, -1)
    both_second = jnp.concatenate([conv2_weight, conv2_probe], 0).reshape(2 * width_one, -1)
    fine = first_layers(
        density, both_first, conv1_bias[:, None], both_second, conv2_bias[:, None]
    ).reshape(span_x, span_y, span_z, 2, width_one)
    pair = jnp.transpose(fine, (3, 0, 1, 2, 4))
    both = cells(pair, lift_weight, 4, "NDHWC")
    extra = cells(pair[:1], lift_probe, 4, "NDHWC")[0]
    hidden, probe = swish_pair(both[0] + lift_bias, both[1] + extra)
    stacked = jnp.stack([hidden.astype(jnp.bfloat16), probe.astype(jnp.bfloat16)])
    tile_shape = stacked.shape[1:4]
    groups = lax.axis_size("sx") * lax.axis_size("sy")
    width = width_three // groups
    blocks = stacked.reshape(2, -1, groups, width)
    blocks = jnp.transpose(blocks, (2, 1, 0, 3)).reshape(groups, -1, 2 * width)
    result = last_layer(
        blocks, flat_weight(conv3_weight), flat_weight(conv3_probe), conv3_bias[:, None], tile_shape
    )
    tx, ty, tz = tile_shape
    result = result.reshape(
        2, -1, tx * lax.axis_size("sx"), ty * lax.axis_size("sy"), tz
    )
    return (result[0], result[1])


def solution(mesh):
    placed = (
        P(None, "sx", "sy", "sz"),
        P(),
        P(),
        P(),
        P(),
        P(),
        P(),
        P(),
        P(),
        P(),
        P(None, None, None, None, ("sx", "sy")),
        P(("sx", "sy")),
        P(None, None, None, None, ("sx", "sy")),
    )
    return jax.shard_map(
        body,
        mesh=mesh,
        in_specs=placed,
        out_specs=(P(("sx", "sy"), None, None, "sz"), P(("sx", "sy"), None, None, "sz")),
        check_vma=False,
    )
```

```python
import functools
import itertools

import jax
import jax.numpy as jnp
from jax import lax
from jax.experimental import pallas as pl
from jax.experimental.pallas import tpu as pltpu
from jax.sharding import PartitionSpec as P

MESH = pl.DeviceIdType.MESH
VMEM = pl.BlockSpec(memory_space=pltpu.VMEM)


def swish_pair(preact, direction):
    sigmoid_value = jax.nn.sigmoid(preact)
    derivative = sigmoid_value * (1.0 + preact * (1.0 - sigmoid_value))
    return (preact * sigmoid_value, derivative * direction)


def cells(volume, weight, stride, out_order):
    return lax.conv_general_dilated(
        volume,
        weight,
        (stride, stride, stride),
        "VALID",
        dimension_numbers=("NDHWC", "ODHWI", out_order),
        preferred_element_type=jnp.float32,
    )


def positions(axes):
    return [lax.axis_index(a) for a in axes], [lax.axis_size(a) for a in axes]


OFFSETS = list(itertools.product((-1, 0, 1), repeat=3))


def upright(row):
    size = row.shape[1]
    same = lax.broadcasted_iota(jnp.int32, (size, size), 0) == lax.broadcasted_iota(
        jnp.int32, (size, size), 1
    )
    return jnp.sum(jnp.where(same, row, 0.0), axis=1, keepdims=True)


def one_hot(rows, columns, source, dim):
    shape = (rows, 1) if dim == 0 else (1, columns)
    want, ok = source(lax.broadcasted_iota(jnp.int32, shape, dim))
    want = jnp.where(ok, want, -1)
    return (lax.broadcasted_iota(jnp.int32, (rows, columns), 1 - dim) == want).astype(jnp.bfloat16)


def tiles_kernel(
    shape, tile, weight1, bias1, weight2, bias2, out, slots, flat, send_sem, recv_sem
):
    width = 2
    channels, span_x, span_y, span_z = shape
    wide_x, wide_y, wide_z = (span + 2 * width for span in (span_x, span_y, span_z))
    axes = ("sx", "sy", "sz")
    at, counts = positions(axes)

    def there(offset):
        ok = None
        for here, step, count in zip(at, offset, counts):
            if step:
                one = (here + step >= 0) & (here + step < count)
                ok = one if ok is None else ok & one
        return ok, tuple(here + step for here, step in zip(at, offset))

    others = [(i, o) for i, o in enumerate(OFFSETS) if any(o)]
    barrier = pltpu.get_barrier_semaphore()
    for _, offset in others:
        ok, target = there(offset)

        @pl.when(ok)
        def _():
            pl.semaphore_signal(barrier, inc=1, device_id=target, device_id_type=MESH)

    peers = 1
    for here, count in zip(at, counts):
        peers *= 1 + (here > 0).astype(jnp.int32) + (here < count - 1).astype(jnp.int32)
    pl.semaphore_wait(barrier, peers - 1)

    def copy(i, offset, target):
        return pltpu.make_async_remote_copy(
            src_ref=tile,
            dst_ref=slots.at[len(OFFSETS) - 1 - i],
            send_sem=send_sem.at[i],
            recv_sem=recv_sem.at[len(OFFSETS) - 1 - i],
            device_id=target,
            device_id_type=MESH,
        )

    for i, offset in others:
        ok, target = there(offset)

        @pl.when(ok)
        def _():
            copy(i, offset, target).start()

    slots[len(OFFSETS) // 2] = tile[...]
    cells_in = span_y * span_z

    def column(at_row):
        block, cell = at_row // cells_in, at_row % cells_in
        y = cell // span_z + width + (block // 3 - 1) * span_y
        z = cell % span_z + width + (block % 3 - 1) * span_z
        return y * wide_z + z, (y >= 0) & (y < wide_y) & (z >= 0) & (z < wide_z)

    def line(at_column):
        block, cell = at_column // (channels * span_x), at_column % (channels * span_x)
        x = cell % span_x + width + (block - 1) * span_x
        return x * deep + cell // span_x, (x >= 0) & (x < wide_x)

    pitch = -(-wide_y * wide_z // 128) * 128
    deep = weight1.shape[1] // 27
    columns = one_hot(9 * cells_in, pitch, column, 0)
    lines = one_hot(deep * wide_x, 3 * channels * span_x, line, 1)
    for i, offset in others:
        ok, target = there(offset)

        @pl.when(ok)
        def _():
            mirror = len(OFFSETS) - 1 - i
            copy(mirror, offset, target).wait_recv()

        @pl.when(jnp.logical_not(ok))
        def _():
            slots[i] = jnp.zeros_like(tile)

    dot = functools.partial(jnp.dot, preferred_element_type=jnp.float32)
    near = jnp.concatenate(
        [jnp.concatenate([slots[9 * i + j] for j in range(9)], axis=1) for i in range(3)], axis=0
    )
    near = dot(near, columns).astype(jnp.bfloat16)
    near = dot(lines, near)
    field = jnp.concatenate([near[deep * x : deep * (x + 1)] for x in range(wide_x)], axis=1)

    def patches(values):
        lanes = values.shape[1]
        taps = []
        for q in range(3):
            for r in range(3):
                shift = -((q - 1) * wide_z + r - 1) % lanes
                taps.append(pltpu.roll(values, shift, 1) if shift else values)
        kept = lanes - 2 * pitch
        return jnp.concatenate(
            [tap[:, p * pitch : p * pitch + kept] for p in range(3) for tap in taps], axis=0
        ).astype(jnp.bfloat16)

    width_one = weight1.shape[0] // 2
    both = dot(weight1[...], patches(field))
    hidden, probe = swish_pair(both[:width_one] + upright(bias1[...]), both[width_one:])
    place = lax.broadcasted_iota(jnp.int32, (1, hidden.shape[1]), 1)
    cell = place % pitch
    inside = None
    for here, count, span, index in zip(
        at, counts, (span_x, span_y, span_z), (place // pitch + 1, cell // wide_z, cell % wide_z)
    ):
        index = index - width + here * span
        one = (index >= 0) & (index < count * span)
        inside = one if inside is None else inside & one
    hidden = patches(jnp.where(inside, hidden, 0.0))
    probe = patches(jnp.where(inside, probe, 0.0))
    both = dot(weight2[...], hidden)
    change = both[width_one:] + dot(weight2[:width_one], probe)
    hidden, probe = swish_pair(both[:width_one] + upright(bias2[...]), change)
    flat[...] = jnp.concatenate([hidden, probe], axis=0).T
    for x in range(span_x):
        for y in range(span_y):
            start = x * pitch + (y + width) * wide_z + width
            to = (x * span_y + y) * span_z
            out[to : to + span_z] = flat[start : start + span_z].astype(jnp.bfloat16)
    for i, offset in others:
        ok, target = there(offset)

        @pl.when(ok)
        def _():
            copy(i, offset, target).wait_send()


def first_layers(tile, weight1, bias1, weight2, bias2):
    channels, span_x, span_y, span_z = tile.shape
    merged = (channels * span_x, span_y * span_z)
    pitch = -(-(span_y + 4) * (span_z + 4) // 128) * 128
    pair_width = weight1.shape[0]
    return pl.pallas_call(
        functools.partial(tiles_kernel, tile.shape),
        out_shape=jax.ShapeDtypeStruct((span_x * span_y * span_z, pair_width), tile.dtype),
        in_specs=[VMEM] * 5,
        out_specs=VMEM,
        scratch_shapes=[
            pltpu.VMEM((len(OFFSETS),) + merged, tile.dtype),
            pltpu.VMEM((span_x * pitch, pair_width), jnp.float32),
            pltpu.SemaphoreType.DMA((len(OFFSETS),)),
            pltpu.SemaphoreType.DMA((len(OFFSETS),)),
        ],
        compiler_params=pltpu.CompilerParams(
            collective_id=0, has_side_effects=True, vmem_limit_bytes=48 * 2**20
        ),
    )(tile.reshape(merged), weight1, bias1, weight2, bias2)


def last_kernel(
    tile_shape, blocks, weight, probe, bias, features, tangents, lifted, sent, rows, copies, parts, landed,
    lift_send, lift_recv, part_send, part_recv,
):
    tx, ty, tz = tile_shape
    (ix, iy, iz), (nx, ny, nz) = positions(("sx", "sy", "sz"))
    groups = nx * ny
    me = ix * ny + iy
    width = weight.shape[0] // 27
    whole_y, depth = ny * ty, tz + 2
    step_y, step_x = depth, depth * (whole_y + 1)
    count = sent.shape[1]
    cellcount, owned = features.shape

    def place(k, dz):
        group = lax.rem(me + k, groups)
        return group, (lax.div(group, ny), lax.rem(group, ny), iz + dz)

    plan = [(dz, k) for dz in (0, -1, 1) for k in range(groups) if k or dz]

    def guarded(dz, action):
        if dz == 0:
            action()
        else:
            pl.when((iz + dz >= 0) & (iz + dz < nz))(action)

    barrier = pltpu.get_barrier_semaphore()

    def greet(dz):
        for k in range(groups):
            if k or dz:
                _, target = place(k, dz)
                pl.semaphore_signal(barrier, inc=1, device_id=target, device_id_type=MESH)

    for dz in (0, -1, 1):
        guarded(dz, functools.partial(greet, dz))
    slabs = 1 + (iz > 0).astype(jnp.int32) + (iz < nz - 1).astype(jnp.int32)
    pl.semaphore_wait(barrier, groups * slabs - 1)

    def lift_copy(dz, k):
        group, target = place(k, dz)
        return pltpu.make_async_remote_copy(
            src_ref=blocks.at[group],
            dst_ref=lifted.at[1 - dz, me],
            send_sem=lift_send.at[1 + dz, k],
            recv_sem=lift_recv.at[1 - dz, me],
            device_id=target,
            device_id_type=MESH,
        )

    def arrival(dz, group):
        return pltpu.make_async_remote_copy(
            src_ref=blocks.at[group],
            dst_ref=lifted.at[1 + dz, group],
            send_sem=lift_send.at[1 + dz, 0],
            recv_sem=lift_recv.at[1 + dz, group],
            device_id=(lax.div(group, ny), lax.rem(group, ny), iz),
            device_id_type=MESH,
        )

    def launch(dz):
        for k in range(groups):
            if k or dz:
                lift_copy(dz, k).start()

    for dz in (0, -1, 1):
        guarded(dz, functools.partial(launch, dz))

    lifted[1, me] = blocks[me]
    rows[...] = jnp.zeros_like(rows)

    def row_of(x, y, z):
        return (x + 1) * step_x + (y + 1) * step_y + z + 1

    def land(dz):
        for k in range(groups):
            if k or dz:
                arrival(dz, lax.rem(me + k, groups)).wait_recv()
        for group in range(groups):
            gx, gy = group // ny, group % ny
            block = lifted[1 + dz, group].astype(jnp.float32)
            for i in range(tx):
                for j in range(ty):
                    start = (i * ty + j) * tz
                    first, size, z = {0: (0, tz, 0), -1: (tz - 1, 1, -1), 1: (0, 1, tz)}[dz]
                    target = row_of(gx * tx + i, gy * ty + j, z)
                    rows[target : target + size, 0 : 2 * width] = block[
                        start + first : start + first + size
                    ]

    for dz in (0, -1, 1):
        guarded(dz, functools.partial(land, dz))

    lanes = rows.shape[1]
    per = lanes // width
    lane = lax.broadcasted_iota(jnp.int32, rows.shape, 1) // width
    full = rows[...]
    for which in range(2):
        for k in range(per):
            shift = (k - which) * width % lanes
            turned = pltpu.roll(full, shift, 1) if shift else full
            copies[which * per + k] = jnp.where(lane == k, turned, 0.0)

    taps = [p * step_x + q * step_y + r for p in range(3) for q in range(3) for r in range(3)]

    def patches(which):
        chunks = []
        for first in range(0, 27, per):
            chunk = None
            for k, tap in enumerate(taps[first : first + per]):
                window = copies[which * per + k, tap : tap + count]
                chunk = window if chunk is None else chunk + window
            chunks.append(chunk.astype(jnp.bfloat16))
        return jnp.concatenate(chunks, axis=1)[:, : 27 * width]

    hidden, change = patches(0), patches(1)
    dot = functools.partial(jnp.dot, preferred_element_type=jnp.float32)
    primal = dot(hidden, weight[...])
    tangent = dot(hidden, probe[...]) + dot(change, weight[...])

    row = lax.broadcasted_iota(jnp.int32, (count, cellcount), 0)
    cell = lax.broadcasted_iota(jnp.int32, (count, cellcount), 1)
    source = (
        cell // (whole_y * tz) * step_x + cell // tz % whole_y * step_y + cell % tz
    )
    pick = (row == source).astype(jnp.bfloat16)
    for which, value in enumerate((primal, tangent)):
        dense = dot(value.T.astype(jnp.bfloat16), pick).astype(jnp.bfloat16)
        for group in range(groups):
            parts[group, which] = dense[group * owned : (group + 1) * owned]

    def part_copy(k):
        group, target = place(k, 0)
        return pltpu.make_async_remote_copy(
            src_ref=parts.at[group],
            dst_ref=landed.at[me],
            send_sem=part_send.at[k],
            recv_sem=part_recv.at[me],
            device_id=target,
            device_id_type=MESH,
        )

    def part_arrival(k):
        group, target = place(k, 0)
        return pltpu.make_async_remote_copy(
            src_ref=parts.at[group],
            dst_ref=landed.at[group],
            send_sem=part_send.at[k],
            recv_sem=part_recv.at[group],
            device_id=target,
            device_id_type=MESH,
        )

    for k in range(1, groups):
        part_copy(k).start()
    total = parts[me].astype(jnp.float32)
    for k in range(1, groups):
        part_arrival(k).wait_recv()
        total = total + landed[lax.rem(me + k, groups)].astype(jnp.float32)
    features[...] = (total[0].T + bias[...]).astype(features.dtype)
    tangents[...] = total[1].T.astype(tangents.dtype)
    for dz, k in plan:
        guarded(dz, lambda: lift_copy(dz, k).wait_send())
    for k in range(1, groups):
        part_copy(k).wait_send()


def last_layer(blocks, weight, probe, bias, tile_shape):
    tx, ty, tz = tile_shape
    (nx, ny) = lax.axis_size("sx"), lax.axis_size("sy")
    groups, cells_in, pair_width = blocks.shape
    width = pair_width // 2
    outputs = weight.shape[1]
    owned = outputs // groups
    step_x = (ny * ty + 1) * (tz + 2)
    count = -(-nx * tx * step_x // 128) * 128
    height = -(-(count + 2 * step_x + 2 * (tz + 2) + 2) // 16) * 16
    cellcount = nx * tx * ny * ty * tz
    lanes = 128
    per = lanes // width
    bf16, f32 = jnp.bfloat16, jnp.float32
    return pl.pallas_call(
        functools.partial(last_kernel, tile_shape),
        out_shape=[jax.ShapeDtypeStruct((cellcount, owned), bf16)] * 2,
        in_specs=[VMEM] * 4,
        out_specs=[VMEM] * 2,
        scratch_shapes=[
            pltpu.VMEM((3, groups, cells_in, pair_width), bf16),
            pltpu.VMEM((1, count, 128), bf16),
            pltpu.VMEM((height, lanes), f32),
            pltpu.VMEM((2 * per, height, lanes), f32),
            pltpu.VMEM((groups, 2, owned, cellcount), bf16),
            pltpu.VMEM((groups, 2, owned, cellcount), bf16),
            pltpu.SemaphoreType.DMA((3, groups)),
            pltpu.SemaphoreType.DMA((3, groups)),
            pltpu.SemaphoreType.DMA((groups,)),
            pltpu.SemaphoreType.DMA((groups,)),
        ],
        compiler_params=pltpu.CompilerParams(
            collective_id=1, has_side_effects=True, vmem_limit_bytes=48 * 2**20
        ),
    )(blocks, weight, probe, bias)


def flat_weight(weight):
    outputs = weight.shape[0]
    return jnp.transpose(weight, (1, 2, 3, 4, 0)).reshape(-1, outputs)


def body(
    density,
    conv1_weight,
    conv1_bias,
    conv1_probe,
    conv2_weight,
    conv2_bias,
    conv2_probe,
    lift_weight,
    lift_bias,
    lift_probe,
    conv3_weight,
    conv3_bias,
    conv3_probe,
):
    channels_in, span_x, span_y, span_z = density.shape
    width_one = conv1_weight.shape[0]
    width_three = lift_weight.shape[0]
    both_first = jnp.concatenate([conv1_weight, conv1_probe], 0)
    spare = -channels_in % 8
    both_first = jnp.pad(both_first, ((0, 0),) * 4 + ((0, spare),)).reshape(2 * width_one, -1)
    both_second = jnp.concatenate([conv2_weight, conv2_probe], 0).reshape(2 * width_one, -1)
    fine = first_layers(
        density, both_first, conv1_bias[None], both_second, conv2_bias[None]
    ).reshape(span_x, span_y, span_z, 2, width_one)
    pair = jnp.transpose(fine, (3, 0, 1, 2, 4))
    both = cells(pair, lift_weight, 4, "NDHWC")
    extra = cells(pair[:1], lift_probe, 4, "NDHWC")[0]
    hidden, probe = swish_pair(both[0] + lift_bias, both[1] + extra)
    stacked = jnp.stack([hidden.astype(jnp.bfloat16), probe.astype(jnp.bfloat16)])
    tile_shape = stacked.shape[1:4]
    groups = lax.axis_size("sx") * lax.axis_size("sy")
    width = width_three // groups
    blocks = stacked.reshape(2, -1, groups, width)
    blocks = jnp.transpose(blocks, (2, 1, 0, 3)).reshape(groups, -1, 2 * width)
    result = last_layer(
        blocks, flat_weight(conv3_weight), flat_weight(conv3_probe), conv3_bias[None], tile_shape
    )
    tx, ty, tz = tile_shape
    shape = (tx * lax.axis_size("sx"), ty * lax.axis_size("sy"), tz, -1)
    return tuple(jnp.transpose(value.reshape(shape), (3, 0, 1, 2)) for value in result)


def solution(mesh):
    placed = (
        P(None, "sx", "sy", "sz"),
        P(),
        P(),
        P(),
        P(),
        P(),
        P(),
        P(),
        P(),
        P(),
        P(None, None, None, None, ("sx", "sy")),
        P(("sx", "sy")),
        P(None, None, None, None, ("sx", "sy")),
    )
    return jax.shard_map(
        body,
        mesh=mesh,
        in_specs=placed,
        out_specs=(P(("sx", "sy"), None, None, "sz"), P(("sx", "sy"), None, None, "sz")),
        check_vma=False,
    )
```

```python
import functools
import itertools

import jax
import jax.numpy as jnp
from jax import lax
from jax.experimental import pallas as pl
from jax.experimental.pallas import tpu as pltpu
from jax.sharding import PartitionSpec as P

MESH = pl.DeviceIdType.MESH
VMEM = pl.BlockSpec(memory_space=pltpu.VMEM)


def swish_pair(preact, direction):
    sigmoid_value = jax.nn.sigmoid(preact)
    derivative = sigmoid_value * (1.0 + preact * (1.0 - sigmoid_value))
    return (preact * sigmoid_value, derivative * direction)


def cells(volume, weight, stride, out_order):
    return lax.conv_general_dilated(
        volume,
        weight,
        (stride, stride, stride),
        "VALID",
        dimension_numbers=("NDHWC", "ODHWI", out_order),
        preferred_element_type=jnp.float32,
    )


def positions(axes):
    return [lax.axis_index(a) for a in axes], [lax.axis_size(a) for a in axes]


OFFSETS = list(itertools.product((-1, 0, 1), repeat=3))


def upright(row):
    size = row.shape[1]
    same = lax.broadcasted_iota(jnp.int32, (size, size), 0) == lax.broadcasted_iota(
        jnp.int32, (size, size), 1
    )
    return jnp.sum(jnp.where(same, row, 0.0), axis=1, keepdims=True)


def one_hot(rows, columns, source, dim):
    shape = (rows, 1) if dim == 0 else (1, columns)
    want, ok = source(lax.broadcasted_iota(jnp.int32, shape, dim))
    want = jnp.where(ok, want, -1)
    return (lax.broadcasted_iota(jnp.int32, (rows, columns), 1 - dim) == want).astype(jnp.bfloat16)


def tiles_kernel(
    shape, tile, weight1, bias1, weight2, probe2, bias2, out, slots, flat, send_sem, recv_sem
):
    width = 2
    channels, span_x, span_y, span_z = shape
    wide_x, wide_y, wide_z = (span + 2 * width for span in (span_x, span_y, span_z))
    axes = ("sx", "sy", "sz")
    at, counts = positions(axes)

    def there(offset):
        ok = None
        for here, step, count in zip(at, offset, counts):
            if step:
                one = (here + step >= 0) & (here + step < count)
                ok = one if ok is None else ok & one
        return ok, tuple(here + step for here, step in zip(at, offset))

    others = [(i, o) for i, o in enumerate(OFFSETS) if any(o)]
    barrier = pltpu.get_barrier_semaphore()
    for _, offset in others:
        ok, target = there(offset)

        @pl.when(ok)
        def _():
            pl.semaphore_signal(barrier, inc=1, device_id=target, device_id_type=MESH)

    peers = 1
    for here, count in zip(at, counts):
        peers *= 1 + (here > 0).astype(jnp.int32) + (here < count - 1).astype(jnp.int32)
    pl.semaphore_wait(barrier, peers - 1)

    def copy(i, offset, target):
        return pltpu.make_async_remote_copy(
            src_ref=tile,
            dst_ref=slots.at[len(OFFSETS) - 1 - i],
            send_sem=send_sem.at[i],
            recv_sem=recv_sem.at[len(OFFSETS) - 1 - i],
            device_id=target,
            device_id_type=MESH,
        )

    for i, offset in others:
        ok, target = there(offset)

        @pl.when(ok)
        def _():
            copy(i, offset, target).start()

    slots[len(OFFSETS) // 2] = tile[...]
    cells_in = span_y * span_z

    def column(at_row):
        block, cell = at_row // cells_in, at_row % cells_in
        y = cell // span_z + width + (block // 3 - 1) * span_y
        z = cell % span_z + width + (block % 3 - 1) * span_z
        return y * wide_z + z, (y >= 0) & (y < wide_y) & (z >= 0) & (z < wide_z)

    def line(at_column):
        block, cell = at_column // (channels * span_x), at_column % (channels * span_x)
        x = cell % span_x + width + (block - 1) * span_x
        return x * deep + cell // span_x, (x >= 0) & (x < wide_x)

    pitch = -(-wide_y * wide_z // 128) * 128
    deep = weight1.shape[1] // 27
    columns = one_hot(9 * cells_in, pitch, column, 0)
    lines = one_hot(deep * wide_x, 3 * channels * span_x, line, 1)
    for i, offset in others:
        ok, target = there(offset)

        @pl.when(ok)
        def _():
            mirror = len(OFFSETS) - 1 - i
            copy(mirror, offset, target).wait_recv()

        @pl.when(jnp.logical_not(ok))
        def _():
            slots[i] = jnp.zeros_like(tile)

    dot = functools.partial(jnp.dot, preferred_element_type=jnp.float32)
    near = jnp.concatenate(
        [jnp.concatenate([slots[9 * i + j] for j in range(9)], axis=1) for i in range(3)], axis=0
    )
    near = dot(near, columns).astype(jnp.bfloat16)
    near = dot(lines, near)
    field = jnp.concatenate([near[deep * x : deep * (x + 1)] for x in range(wide_x)], axis=1)

    def patches(values):
        lanes = values.shape[1]
        taps = []
        for q in range(3):
            for r in range(3):
                shift = -((q - 1) * wide_z + r - 1) % lanes
                taps.append(pltpu.roll(values, shift, 1) if shift else values)
        kept = lanes - 2 * pitch
        return jnp.concatenate(
            [tap[:, p * pitch : p * pitch + kept] for p in range(3) for tap in taps], axis=0
        ).astype(jnp.bfloat16)

    width_one = weight1.shape[0] // 2
    both = dot(weight1[...], patches(field))
    hidden, probe = swish_pair(both[:width_one] + upright(bias1[...]), both[width_one:])
    place = lax.broadcasted_iota(jnp.int32, (1, hidden.shape[1]), 1)
    cell = place % pitch
    inside = None
    for here, count, span, index in zip(
        at, counts, (span_x, span_y, span_z), (place // pitch + 1, cell // wide_z, cell % wide_z)
    ):
        index = index - width + here * span
        one = (index >= 0) & (index < count * span)
        inside = one if inside is None else inside & one
    hidden = patches(jnp.where(inside, hidden, 0.0))
    probe = patches(jnp.where(inside, probe, 0.0))
    change = dot(probe2[...], hidden) + dot(weight2[...], probe)
    hidden, probe = swish_pair(dot(weight2[...], hidden) + upright(bias2[...]), change)
    flat[...] = jnp.concatenate([hidden, probe], axis=0).T
    for x in range(span_x):
        for y in range(span_y):
            start = x * pitch + (y + width) * wide_z + width
            to = (x * span_y + y) * span_z
            out[to : to + span_z] = flat[start : start + span_z].astype(jnp.bfloat16)
    for i, offset in others:
        ok, target = there(offset)

        @pl.when(ok)
        def _():
            copy(i, offset, target).wait_send()


def first_layers(tile, weight1, bias1, weight2, probe2, bias2):
    channels, span_x, span_y, span_z = tile.shape
    merged = (channels * span_x, span_y * span_z)
    pitch = -(-(span_y + 4) * (span_z + 4) // 128) * 128
    pair_width = weight1.shape[0]
    return pl.pallas_call(
        functools.partial(tiles_kernel, tile.shape),
        out_shape=jax.ShapeDtypeStruct((span_x * span_y * span_z, pair_width), tile.dtype),
        in_specs=[VMEM] * 6,
        out_specs=VMEM,
        scratch_shapes=[
            pltpu.VMEM((len(OFFSETS),) + merged, tile.dtype),
            pltpu.VMEM((span_x * pitch, pair_width), jnp.float32),
            pltpu.SemaphoreType.DMA((len(OFFSETS),)),
            pltpu.SemaphoreType.DMA((len(OFFSETS),)),
        ],
        compiler_params=pltpu.CompilerParams(
            collective_id=0, has_side_effects=True, vmem_limit_bytes=48 * 2**20
        ),
    )(tile.reshape(merged), weight1, bias1, weight2, probe2, bias2)


def last_kernel(
    tile_shape, blocks, weight, probe, bias, features, tangents, lifted, sent, rows, copies, parts, landed,
    lift_send, lift_recv, part_send, part_recv,
):
    tx, ty, tz = tile_shape
    (ix, iy, iz), (nx, ny, nz) = positions(("sx", "sy", "sz"))
    groups = nx * ny
    me = ix * ny + iy
    width = weight.shape[0] // 27
    whole_y, depth = ny * ty, tz + 2
    step_y, step_x = depth, depth * (whole_y + 1)
    count = sent.shape[1]
    cellcount, owned = features.shape

    def place(k, dz):
        group = lax.rem(me + k, groups)
        return group, (lax.div(group, ny), lax.rem(group, ny), iz + dz)

    plan = [(dz, k) for dz in (0, -1, 1) for k in range(groups) if k or dz]

    def guarded(dz, action):
        if dz == 0:
            action()
        else:
            pl.when((iz + dz >= 0) & (iz + dz < nz))(action)

    barrier = pltpu.get_barrier_semaphore()

    def greet(dz):
        for k in range(groups):
            if k or dz:
                _, target = place(k, dz)
                pl.semaphore_signal(barrier, inc=1, device_id=target, device_id_type=MESH)

    for dz in (0, -1, 1):
        guarded(dz, functools.partial(greet, dz))
    slabs = 1 + (iz > 0).astype(jnp.int32) + (iz < nz - 1).astype(jnp.int32)
    pl.semaphore_wait(barrier, groups * slabs - 1)

    def lift_copy(dz, k):
        group, target = place(k, dz)
        return pltpu.make_async_remote_copy(
            src_ref=blocks.at[group],
            dst_ref=lifted.at[1 - dz, me],
            send_sem=lift_send.at[1 + dz, k],
            recv_sem=lift_recv.at[1 - dz, me],
            device_id=target,
            device_id_type=MESH,
        )

    def arrival(dz, group):
        return pltpu.make_async_remote_copy(
            src_ref=blocks.at[group],
            dst_ref=lifted.at[1 + dz, group],
            send_sem=lift_send.at[1 + dz, 0],
            recv_sem=lift_recv.at[1 + dz, group],
            device_id=(lax.div(group, ny), lax.rem(group, ny), iz),
            device_id_type=MESH,
        )

    def launch(dz):
        for k in range(groups):
            if k or dz:
                lift_copy(dz, k).start()

    for dz in (0, -1, 1):
        guarded(dz, functools.partial(launch, dz))

    lifted[1, me] = blocks[me]
    rows[...] = jnp.zeros_like(rows)

    def row_of(x, y, z):
        return (x + 1) * step_x + (y + 1) * step_y + z + 1

    def land(dz):
        for k in range(groups):
            if k or dz:
                arrival(dz, lax.rem(me + k, groups)).wait_recv()
        for group in range(groups):
            gx, gy = group // ny, group % ny
            block = lifted[1 + dz, group].astype(jnp.float32)
            for i in range(tx):
                for j in range(ty):
                    start = (i * ty + j) * tz
                    first, size, z = {0: (0, tz, 0), -1: (tz - 1, 1, -1), 1: (0, 1, tz)}[dz]
                    target = row_of(gx * tx + i, gy * ty + j, z)
                    rows[target : target + size, 0 : 2 * width] = block[
                        start + first : start + first + size
                    ]

    for dz in (0, -1, 1):
        guarded(dz, functools.partial(land, dz))

    lanes = rows.shape[1]
    per = lanes // width
    lane = lax.broadcasted_iota(jnp.int32, rows.shape, 1) // width
    full = rows[...]
    for which in range(2):
        for k in range(per):
            shift = (k - which) * width % lanes
            turned = pltpu.roll(full, shift, 1) if shift else full
            copies[which * per + k] = jnp.where(lane == k, turned, 0.0)

    taps = [p * step_x + q * step_y + r for p in range(3) for q in range(3) for r in range(3)]

    def patches(which):
        chunks = []
        for first in range(0, 27, per):
            chunk = None
            for k, tap in enumerate(taps[first : first + per]):
                window = copies[which * per + k, tap : tap + count]
                chunk = window if chunk is None else chunk + window
            chunks.append(chunk.astype(jnp.bfloat16))
        return jnp.concatenate(chunks, axis=1)[:, : 27 * width]

    hidden, change = patches(0), patches(1)
    dot = functools.partial(jnp.dot, preferred_element_type=jnp.float32)
    primal = dot(hidden, weight[...])
    tangent = dot(hidden, probe[...]) + dot(change, weight[...])

    row = lax.broadcasted_iota(jnp.int32, (count, cellcount), 0)
    cell = lax.broadcasted_iota(jnp.int32, (count, cellcount), 1)
    source = (
        cell // (whole_y * tz) * step_x + cell // tz % whole_y * step_y + cell % tz
    )
    pick = (row == source).astype(jnp.bfloat16)
    for which, value in enumerate((primal, tangent)):
        dense = dot(value.T.astype(jnp.bfloat16), pick).astype(jnp.bfloat16)
        for group in range(groups):
            parts[group, which] = dense[group * owned : (group + 1) * owned]

    def part_copy(k):
        group, target = place(k, 0)
        return pltpu.make_async_remote_copy(
            src_ref=parts.at[group],
            dst_ref=landed.at[me],
            send_sem=part_send.at[k],
            recv_sem=part_recv.at[me],
            device_id=target,
            device_id_type=MESH,
        )

    def part_arrival(k):
        group, target = place(k, 0)
        return pltpu.make_async_remote_copy(
            src_ref=parts.at[group],
            dst_ref=landed.at[group],
            send_sem=part_send.at[k],
            recv_sem=part_recv.at[group],
            device_id=target,
            device_id_type=MESH,
        )

    for k in range(1, groups):
        part_copy(k).start()
    total = parts[me].astype(jnp.float32)
    for k in range(1, groups):
        part_arrival(k).wait_recv()
        total = total + landed[lax.rem(me + k, groups)].astype(jnp.float32)
    features[...] = (total[0].T + bias[...]).astype(features.dtype)
    tangents[...] = total[1].T.astype(tangents.dtype)
    for dz, k in plan:
        guarded(dz, lambda: lift_copy(dz, k).wait_send())
    for k in range(1, groups):
        part_copy(k).wait_send()


def last_layer(blocks, weight, probe, bias, tile_shape):
    tx, ty, tz = tile_shape
    (nx, ny) = lax.axis_size("sx"), lax.axis_size("sy")
    groups, cells_in, pair_width = blocks.shape
    width = pair_width // 2
    outputs = weight.shape[1]
    owned = outputs // groups
    step_x = (ny * ty + 1) * (tz + 2)
    count = -(-nx * tx * step_x // 128) * 128
    height = -(-(count + 2 * step_x + 2 * (tz + 2) + 2) // 16) * 16
    cellcount = nx * tx * ny * ty * tz
    lanes = 128
    per = lanes // width
    bf16, f32 = jnp.bfloat16, jnp.float32
    return pl.pallas_call(
        functools.partial(last_kernel, tile_shape),
        out_shape=[jax.ShapeDtypeStruct((cellcount, owned), bf16)] * 2,
        in_specs=[VMEM] * 4,
        out_specs=[VMEM] * 2,
        scratch_shapes=[
            pltpu.VMEM((3, groups, cells_in, pair_width), bf16),
            pltpu.VMEM((1, count, 128), bf16),
            pltpu.VMEM((height, lanes), f32),
            pltpu.VMEM((2 * per, height, lanes), f32),
            pltpu.VMEM((groups, 2, owned, cellcount), bf16),
            pltpu.VMEM((groups, 2, owned, cellcount), bf16),
            pltpu.SemaphoreType.DMA((3, groups)),
            pltpu.SemaphoreType.DMA((3, groups)),
            pltpu.SemaphoreType.DMA((groups,)),
            pltpu.SemaphoreType.DMA((groups,)),
        ],
        compiler_params=pltpu.CompilerParams(
            collective_id=1, has_side_effects=True, vmem_limit_bytes=48 * 2**20
        ),
    )(blocks, weight, probe, bias)


def flat_weight(weight):
    outputs = weight.shape[0]
    return jnp.transpose(weight, (1, 2, 3, 4, 0)).reshape(-1, outputs)


def body(
    density,
    conv1_weight,
    conv1_bias,
    conv1_probe,
    conv2_weight,
    conv2_bias,
    conv2_probe,
    lift_weight,
    lift_bias,
    lift_probe,
    conv3_weight,
    conv3_bias,
    conv3_probe,
):
    channels_in, span_x, span_y, span_z = density.shape
    width_one = conv1_weight.shape[0]
    width_three = lift_weight.shape[0]
    both_first = jnp.concatenate([conv1_weight, conv1_probe], 0)
    spare = -channels_in % 8
    both_first = jnp.pad(both_first, ((0, 0),) * 4 + ((0, spare),)).reshape(2 * width_one, -1)
    fine = first_layers(
        density,
        both_first,
        conv1_bias[None],
        conv2_weight.reshape(width_one, -1),
        conv2_probe.reshape(width_one, -1),
        conv2_bias[None],
    ).reshape(span_x, span_y, span_z, 2, width_one)
    pair = jnp.transpose(fine, (3, 0, 1, 2, 4))
    both = cells(pair, lift_weight, 4, "NDHWC")
    extra = cells(pair[:1], lift_probe, 4, "NDHWC")[0]
    hidden, probe = swish_pair(both[0] + lift_bias, both[1] + extra)
    stacked = jnp.stack([hidden.astype(jnp.bfloat16), probe.astype(jnp.bfloat16)])
    tile_shape = stacked.shape[1:4]
    groups = lax.axis_size("sx") * lax.axis_size("sy")
    width = width_three // groups
    blocks = stacked.reshape(2, -1, groups, width)
    blocks = jnp.transpose(blocks, (2, 1, 0, 3)).reshape(groups, -1, 2 * width)
    result = last_layer(
        blocks, flat_weight(conv3_weight), flat_weight(conv3_probe), conv3_bias[None], tile_shape
    )
    tx, ty, tz = tile_shape
    shape = (tx * lax.axis_size("sx"), ty * lax.axis_size("sy"), tz, -1)
    return tuple(jnp.transpose(value.reshape(shape), (3, 0, 1, 2)) for value in result)


def solution(mesh):
    placed = (
        P(None, "sx", "sy", "sz"),
        P(),
        P(),
        P(),
        P(),
        P(),
        P(),
        P(),
        P(),
        P(),
        P(None, None, None, None, ("sx", "sy")),
        P(("sx", "sy")),
        P(None, None, None, None, ("sx", "sy")),
    )
    return jax.shard_map(
        body,
        mesh=mesh,
        in_specs=placed,
        out_specs=(P(("sx", "sy"), None, None, "sz"), P(("sx", "sy"), None, None, "sz")),
        check_vma=False,
    )
```
